32 devices in a mesh: pipe: 8 (over z, x), dp: 4 (over y, core).
Axes of the slice: x: 2, y: 2, z: 4, core: 2. Of those that a mesh axis runs over, the one named last changes fastest.
Arguments:
- kept_down_first: bfloat16 [8, 256, 6144], P('pipe', 'dp'), may hold values from -6 to 6
- kept_up_first: bfloat16 [8, 256, 6144], P('pipe', 'dp'), may hold values from -6 to 6
- kept_down_second: bfloat16 [8, 256, 6144], P('pipe', 'dp'), may hold values from -6 to 6
- kept_up_second: bfloat16 [8, 256, 6144], P('pipe', 'dp'), may hold values from -6 to 6
- cot_down: bfloat16 [8, 256, 6144], P('pipe', 'dp'), may hold values from -6 to 6
- cot_up: bfloat16 [8, 256, 6144], P('pipe', 'dp'), may hold values from -6 to 6
- loss_down: bfloat16 [256, 6144], P('dp'), may hold values from -6 to 6
- loss_up: bfloat16 [256, 6144], P('dp'), may hold values from -6 to 6
- section_a: bfloat16 [8, 6144, 32], P('pipe')
- section_b: bfloat16 [8, 32, 6144], P('pipe')
- mirror_a: bfloat16 [8, 6144, 32], P('pipe'), as said below
- mirror_b: bfloat16 [8, 32, 6144], P('pipe')
Outputs:
- grad_a: float32 [8, 6144, 32], P('pipe', 'dp')
- grad_b: float32 [8, 32, 6144], P('pipe', None, 'dp')
The draws below stay inside these ranges and needn't reach their ends.
Inputs may be any that keep to these rules, and one draw needn't show every extreme that they name: mirror_a[j] equals section_a[7-j] and mirror_b[j] equals section_b[7-j].
All inputs are finite; a program needn't handle non-finite values.
Results may differ from the reference program's by a relative error of at most 0.0051.
Values may be sent and summed in bfloat16 or wider, within the bound.
A program may use at most 64 MiB of HBM per device.

```python
import jax
import jax.numpy as jnp
from jax import lax

D = 6144
RANK = 32
ROWS = 256
SECTIONS = 8


def table_a(key):
    inner = jax.random.fold_in(key, 11)
    return jax.random.normal(inner, (SECTIONS, D, RANK), jnp.float32) * D ** (-0.5)


def table_b(key):
    inner = jax.random.fold_in(key, 12)
    return jax.random.normal(inner, (SECTIONS, RANK, D), jnp.float32) * RANK ** (-0.5)


def draw_section_a(key, part):
    shared = table_a(key)
    return shared.astype(jnp.bfloat16)


def draw_section_b(key, part):
    shared = table_b(key)
    return shared.astype(jnp.bfloat16)


def draw_mirror_a(key, part):
    shared = table_a(key)
    return jnp.flip(shared, axis=0).astype(jnp.bfloat16)


def draw_mirror_b(key, part):
    shared = table_b(key)
    return jnp.flip(shared, axis=0).astype(jnp.bfloat16)


def with_spikes(drawn, own_key, source, target, blocks, factor):
    owner, partner = [(jnp.arange(drawn.shape[position]) // (drawn.shape[position] // blocks)).reshape([-1 if axis == position else 1 for axis in range(drawn.ndim)]) for position in (source, target)]
    chosen = jax.random.permutation(own_key, blocks)[partner]
    strong = (owner == chosen) | (owner == (partner + blocks // 2) % blocks)
    return jnp.where(strong, factor * drawn, drawn)


def block_levels(own_key, shape, split, smallest, high):
    def one(axis_at, shards_of):
        steps = jax.random.uniform(jax.random.fold_in(jax.random.fold_in(own_key, 6), axis_at), (shards_of,), jnp.float32, smallest / len(split), high / len(split))
        return jnp.repeat(jnp.exp(steps), shape[axis_at] // shards_of).reshape((-1,) + (1,) * (len(shape) - axis_at - 1))

    factor_of = one(*split[0])
    for cut in split[1:]:
        factor_of = factor_of * one(*cut)
    return factor_of


def normal_values(stream_key, shape, scale, limit, split=(), kind=jnp.bfloat16):
    entries = scale * jax.random.normal(stream_key, shape, jnp.float32)
    if split:
        entries = entries * block_levels(stream_key, shape, split, -0.22, 0.18)
    return jnp.clip(entries, -limit, limit).astype(kind)


def heavy_noise(own_key, dims, deviation, limit, shards, heavy, kind=jnp.bfloat16):
    array = deviation * jax.random.normal(own_key, dims, jnp.float32)
    if shards:
        array = array * block_levels(own_key, dims, shards, -0.22, 0.18)
    return jnp.clip(with_spikes(array, jax.random.fold_in(own_key, 3), *heavy), -limit, limit).astype(kind)


def setup_inputs(seed: int = 0) -> dict:
    key_of = jax.random.split(jax.random.key(seed), 13)
    return {
        "kept_down_first": normal_values(key_of[0], (SECTIONS, ROWS, D), 1.0, 6.0, ((0, 8), (1, 4))),
        "kept_up_first": normal_values(key_of[1], (SECTIONS, ROWS, D), 1.0, 6.0, ((0, 8), (1, 4))),
        "kept_down_second": normal_values(key_of[2], (SECTIONS, ROWS, D), 1.0, 6.0, ((0, 8), (1, 4))),
        "kept_up_second": normal_values(key_of[3], (SECTIONS, ROWS, D), 1.0, 6.0, ((0, 8), (1, 4))),
        "cot_down": heavy_noise(key_of[4], (SECTIONS, ROWS, D), 1.0, 6.0, ((0, 8), (1, 4)), (1, 2, 4, 2.0)),
        "cot_up": heavy_noise(key_of[5], (SECTIONS, ROWS, D), 1.0, 6.0, ((0, 8), (1, 4)), (1, 2, 4, 2.0)),
        "loss_down": normal_values(key_of[6], (ROWS, D), 1.0, 6.0, ((0, 4),)),
        "loss_up": normal_values(key_of[7], (ROWS, D), 1.0, 6.0, ((0, 4),)),
        "section_a": draw_section_a(jax.random.fold_in(key_of[12], 71), 0),
        "section_b": draw_section_b(jax.random.fold_in(key_of[12], 71), 0),
        "mirror_a": draw_mirror_a(jax.random.fold_in(key_of[12], 71), 0),
        "mirror_b": draw_mirror_b(jax.random.fold_in(key_of[12], 71), 0),
    }


EPS = 1e-06

def section_back(inputs, grad_out, proj_a, proj_b):
    values = inputs.astype(jnp.float32)
    inverse = lax.rsqrt(lax.optimization_barrier(jnp.mean(values * values, axis=-1, keepdims=True)) + EPS)
    normed = values * inverse
    normed_b = normed.astype(jnp.bfloat16)
    pre = jnp.dot(normed_b, proj_a, preferred_element_type=jnp.float32)
    sigma = jax.nn.sigmoid(pre)
    hidden = (pre * sigma).astype(jnp.bfloat16)
    grad_b = jnp.dot(hidden.T, grad_out, preferred_element_type=jnp.float32)
    grad_hidden = jnp.dot(grad_out, proj_b.T, preferred_element_type=jnp.float32)
    grad_pre = (grad_hidden * sigma * (1.0 + pre * (1.0 - sigma))).astype(jnp.bfloat16)
    grad_a = jnp.dot(normed_b.T, grad_pre, preferred_element_type=jnp.float32)
    grad_norm = jnp.dot(grad_pre, proj_a.T, preferred_element_type=jnp.float32)
    inner = lax.optimization_barrier(jnp.mean(grad_norm * normed, axis=-1, keepdims=True))
    grad_in = grad_out.astype(jnp.float32) + inverse * (grad_norm - normed * inner)
    return (grad_in.astype(jnp.bfloat16), grad_a, grad_b)

def run_sections(inputs, grads, proj_a, proj_b):
    return lax.map(lambda item: section_back(item[0], item[1], item[2], item[3]), (inputs, grads, proj_a, proj_b))

def reference(kept_down_first, kept_up_first, kept_down_second, kept_up_second, cot_down, cot_up, loss_down, loss_up, section_a, section_b, mirror_a, mirror_b):
    down_dx, down_a1, down_b1 = run_sections(kept_down_first, cot_down, section_a, section_b)
    up_dx, up_a1, up_b1 = run_sections(kept_up_first, cot_up, mirror_a, mirror_b)
    second_down = jnp.concatenate([down_dx[1:], loss_down[None]], axis=0)
    second_up = jnp.concatenate([loss_up[None], up_dx[:-1]], axis=0)
    unused_d, down_a2, down_b2 = run_sections(kept_down_second, second_down, section_a, section_b)
    unused_u, up_a2, up_b2 = run_sections(kept_up_second, second_up, mirror_a, mirror_b)
    factor = 1.0 / jnp.sqrt(jnp.float32(ROWS))
    grad_a = (down_a1 + down_a2 + jnp.flip(up_a1 + up_a2, axis=0)) * factor
    grad_b = (down_b1 + down_b2 + jnp.flip(up_b1 + up_b2, axis=0)) * factor
    return (grad_a, grad_b)
```

```python
import functools

import jax
import jax.numpy as jnp
from jax import lax
from jax.experimental import pallas as pl
from jax.experimental.pallas import tpu as pltpu
from jax.sharding import PartitionSpec as P

EPS = 1e-06
F32 = jnp.float32
BF16 = jnp.bfloat16


def dot_nt(a, b):
    return lax.dot_general(a, b, (((1,), (1,)), ((), ())), preferred_element_type=F32)


def dot_nn(a, b):
    return lax.dot_general(a, b, (((1,), (0,)), ((), ())), preferred_element_type=F32)


def dot_tn(a, b):
    return lax.dot_general(a, b, (((0,), (0,)), ((), ())), preferred_element_type=F32)


def kernel(
    n,
    m,
    kdf,
    kuf,
    kds,
    kus,
    cd,
    cu,
    ld,
    lu,
    sa,
    sb,
    ma,
    mb,
    ga,
    gb,
    x1,
    x2,
    g1,
    ls,
    wa,
    wb,
    nb,
    dxb,
    hs,
    hr,
    gs,
    gr,
    bp,
    br,
    b2,
    br2,
    ap,
    ar,
    a2,
    ar2,
    rs,
    rr,
    ms,
    mr,
    loc,
    snd,
    rcv,
):
    rows, width = x1.shape[1:]
    rank = wa.shape[1]
    chunk = width // m
    half = width // 2
    hm = m // 2
    tile = min(chunk, 768)
    tiles = width // tile
    per = chunk // tile
    factor = 1.0 / float(rows * m) ** 0.5

    j = lax.axis_index("pipe")
    d = lax.axis_index("dp")
    par = lax.rem(d, 2)
    kk = lax.div(d, 2)
    up = lax.rem(j + 1, n)
    down = lax.rem(j + n - 1, n)
    mirror = n - 1 - j
    pair = (j, d + 1 - 2 * par)
    ahead, behind, across = (up, d), (down, d), (mirror, d)

    def peer(q):
        return lax.rem(kk + q, hm)

    loads = {}
    for at, (src, dst) in enumerate(
        (
            (kds, x2.at[0]),
            (sa, wa.at[0]),
            (kus, x2.at[1]),
            (ma, wa.at[1]),
            (kdf, x1.at[0]),
            (cd, g1.at[0]),
            (sb, wb.at[0]),
            (kuf, x1.at[1]),
            (cu, g1.at[1]),
            (mb, wb.at[1]),
            (ld, ls.at[0]),
            (lu, ls.at[1]),
        )
    ):
        loads[at] = pltpu.make_async_copy(src, dst, loc.at[at])
        loads[at].start()

    barrier = pltpu.get_barrier_semaphore()
    greeted = [ahead, behind, across, pair]
    greeted += [(j, peer(q) * 2 + par) for q in range(1, hm)]
    for other in greeted:
        pl.semaphore_signal(
            barrier, inc=1, device_id=other, device_id_type=pl.DeviceIdType.MESH
        )
    pl.semaphore_wait(barrier, len(greeted))

    def send(slot, src, dst, target):
        copy = pltpu.make_async_remote_copy(
            src_ref=src,
            dst_ref=dst,
            send_sem=snd.at[slot],
            recv_sem=rcv.at[slot],
            device_id=target,
            device_id_type=pl.DeviceIdType.MESH,
        )
        copy.start()
        return copy

    mine = pl.ds(pl.multiple_of(par * half, 128), half)
    toward = (ahead, behind)
    back = (behind, ahead)
    halves = [
        send(w, src.at[:, mine], nb.at[w, par], toward[w])
        for w, src in enumerate((sb, mb))
    ]

    def cols(t):
        return pl.ds(pl.multiple_of(t * tile, 128), tile)

    def square_sum(x):
        xf = x.astype(F32)
        return jnp.sum(xf * xf, axis=-1, keepdims=True)

    zero_r = jnp.zeros((rows, rank), F32)
    zero_1 = jnp.zeros((rows, 1), F32)

    inverse2, pre2 = [], []
    hidden_copies = []
    for w in range(2):
        loads[2 * w].wait()
        loads[2 * w + 1].wait()

        def forward(t, carry, w=w):
            ss, xa = carry
            x = x2[w, :, cols(t)]
            return ss + square_sum(x), xa + dot_nt(x, wa[w, :, cols(t)])

        ss, xa = lax.fori_loop(0, tiles, forward, (zero_1, zero_r))
        inv = lax.rsqrt(ss / width + EPS)
        pre = xa * inv
        inverse2.append(inv)
        pre2.append(pre)
        h = pre * jax.nn.sigmoid(pre)
        hs[w] = jnp.concatenate([h] * (128 // rank), axis=1).astype(BF16)
        hidden_copies.append(send(4 + w, hs.at[w], hr.at[w], toward[w]))

    first = []
    for w in range(2):
        for at in range(3):
            loads[4 + 3 * w + at].wait()

        def project(t, carry, w=w):
            ss, xa, gh = carry
            x = x1[w, :, cols(t)]
            return (
                ss + square_sum(x),
                xa + dot_nt(x, wa[w, :, cols(t)]),
                gh + dot_nt(g1[w, :, cols(t)], wb[w, :, cols(t)]),
            )

        ss, xa, gh = lax.fori_loop(0, tiles, project, (zero_1, zero_r, zero_r))
        inv = lax.rsqrt(ss / width + EPS)
        pre = xa * inv
        sg = jax.nn.sigmoid(pre)
        h = (pre * sg).astype(BF16)
        dp = gh * sg * (1.0 + pre * (1.0 - sg))
        dpb = dp.astype(BF16)
        inner = jnp.sum(dpb.astype(F32) * pre, axis=-1, keepdims=True) / width
        first.append((inv, h, dpb, inv * inv * inner, (dp * inv).astype(BF16)))

    passed = []
    for w in range(2):
        halves[w].wait_recv()
        passed.append(send(2 + w, nb.at[w, par], nb.at[w, par], pair))
    loads[10].wait()
    loads[11].wait()
    edge = (j == 0, j == n - 1)

    returned = []
    for w in range(2):
        inv, h, dpb, scale, wdp = first[w]
        passed[w].wait_recv()

        def cotangent(t, gh, w=w, inv=inv, dpb=dpb, scale=scale):
            e = dot_nn(dpb, wa[w, :, cols(t)])
            dx = (
                g1[w, :, cols(t)].astype(F32)
                + inv * e
                - x1[w, :, cols(t)].astype(F32) * scale
            )
            dx = jnp.where(edge[w], ls[w, :, cols(t)].astype(F32), dx).astype(BF16)
            dxb[w, :, cols(t)] = dx
            side = lax.div(t, tiles // 2)
            at = lax.rem(t, tiles // 2)
            return gh + dot_nt(dx, nb[w, side, :, cols(at)])

        gh = lax.fori_loop(0, tiles, cotangent, zero_r)
        gs[w] = jnp.concatenate([gh] * (128 // rank), axis=1)
        returned.append(send(6 + w, gs.at[w], gr.at[w], back[w]))

    def place(t):
        k = lax.div(t, per)
        at = pl.ds(pl.multiple_of(lax.rem(t, per) * tile, 128), tile)
        return lax.rem(k, 2), lax.div(k, 2), at

    for w in range(2):
        hidden_copies[w].wait_recv()
        inv, h, dpb, scale, wdp = first[w]
        h_next = hr[w][:, :rank]

        def grads_b(t, carry, w=w, h=h, h_next=h_next):
            odd, k, at = place(t)
            bp[odd, k, w, :, at] = dot_tn(h, g1[w, :, cols(t)]).astype(BF16)
            bp[odd, k, 2 + w, :, at] = dot_tn(h_next, dxb[w, :, cols(t)]).astype(BF16)
            return carry

        lax.fori_loop(0, tiles, grads_b, 0)
    b_one = send(8, bp.at[1 - par], br, pair)

    for w in range(2):
        returned[w].wait_recv()
        gh = gr[w][:, :rank]
        pre = pre2[w]
        sg = jax.nn.sigmoid(pre)
        wdp2 = (gh * sg * (1.0 + pre * (1.0 - sg)) * inverse2[w]).astype(BF16)
        wdp1 = first[w][4]

        def grads_a(t, carry, w=w, wdp1=wdp1, wdp2=wdp2):
            odd, k, at = place(t)
            total = dot_tn(wdp1, x1[w, :, cols(t)]) + dot_tn(wdp2, x2[w, :, cols(t)])
            ap[odd, k, w, :, at] = total.astype(BF16)
            return carry

        lax.fori_loop(0, tiles, grads_a, 0)
    a_one = send(9, ap.at[1 - par], ar, pair)

    def added(part, other, total, k, items):
        def body(i, carry):
            total[k, i] = (part[par, k, i].astype(F32) + other[k, i].astype(F32)).astype(BF16)
            return carry

        lax.fori_loop(0, items, body, 0)

    b_one.wait_recv()
    b_two = []
    for q in range(1, hm):
        added(bp, br, b2, peer(q), 4)
        b_two.append(
            send(13 + q, b2.at[peer(q)], br2.at[q - 1], (j, peer(q) * 2 + par))
        )
    a_one.wait_recv()
    a_two = []
    for q in range(1, hm):
        added(ap, ar, a2, peer(q), 2)
        a_two.append(
            send(
                12 + hm + q, a2.at[peer(q)], ar2.at[q - 1], (j, peer(q) * 2 + par)
            )
        )

    def final(part, other, arrived, i):
        total = part[par, kk, i].astype(F32) + other[kk, i].astype(F32)
        for q in range(1, hm):
            total = total + arrived[q - 1, i].astype(F32)
        return total

    for copy in b_two:
        copy.wait_recv()
    rings = []
    for w in range(2):
        rs[w] = final(bp, br, br2, 2 + w).astype(BF16)
        rings.append(send(10 + w, rs.at[w], rr.at[w], back[w]))
    for copy in a_two:
        copy.wait_recv()
    ms[0] = final(ap, ar, ar2, 1).astype(BF16)
    mirror_a = send(12, ms.at[0], mr.at[0], across)
    rings[1].wait_recv()
    ms[1] = (final(bp, br, br2, 1) + rr[1].astype(F32)).astype(BF16)
    mirror_b = send(13, ms.at[1], mr.at[1], across)
    own_a = final(ap, ar, ar2, 0)
    ga[...] = own_a
    rings[0].wait_recv()
    gb[...] = final(bp, br, br2, 0) + rr[0].astype(F32)
    mirror_a.wait_recv()
    ga[...] = (ga[...] + mr[0].astype(F32)) * factor
    mirror_b.wait_recv()
    gb[...] = (gb[...] + mr[1].astype(F32)) * factor

    started = halves + passed + hidden_copies + returned + b_two + a_two + rings
    for copy in started + [b_one, a_one, mirror_a, mirror_b]:
        copy.wait_send()


def per_device(n, m, *args):
    flat = [a if a.ndim == 2 else a[0] for a in args]
    for at in (8, 10):
        flat[at] = flat[at].T
    rows, width = flat[0].shape
    rank = flat[8].shape[0]
    chunk = width // m
    hm = m // 2
    copies = 14 + 2 * (hm - 1)

    def vmem(*shape, dtype=BF16):
        return pltpu.VMEM(shape, dtype)

    grad_a, grad_b = pl.pallas_call(
        functools.partial(kernel, n, m),
        out_shape=[jax.ShapeDtypeStruct((rank, chunk), F32)] * 2,
        in_specs=[pl.BlockSpec(memory_space=pltpu.HBM)] * 12,
        out_specs=[pl.BlockSpec(memory_space=pltpu.VMEM)] * 2,
        scratch_shapes=[
            vmem(2, rows, width),
            vmem(2, rows, width),
            vmem(2, rows, width),
            vmem(2, rows, width),
            vmem(2, rank, width),
            vmem(2, rank, width),
            vmem(2, 2, rank, width // 2),
            vmem(2, rows, width),
            vmem(2, rows, 128),
            vmem(2, rows, 128),
            vmem(2, rows, 128, dtype=F32),
            vmem(2, rows, 128, dtype=F32),
            vmem(2, hm, 4, rank, chunk),
            vmem(hm, 4, rank, chunk),
            vmem(hm, 4, rank, chunk),
            vmem(hm - 1, 4, rank, chunk),
            vmem(2, hm, 2, rank, chunk),
            vmem(hm, 2, rank, chunk),
            vmem(hm, 2, rank, chunk),
            vmem(hm - 1, 2, rank, chunk),
            vmem(2, rank, chunk),
            vmem(2, rank, chunk),
            vmem(2, rank, chunk),
            vmem(2, rank, chunk),
            pltpu.SemaphoreType.DMA((12,)),
            pltpu.SemaphoreType.DMA((copies,)),
            pltpu.SemaphoreType.DMA((copies,)),
        ],
        compiler_params=pltpu.CompilerParams(
            collective_id=0, has_side_effects=True, vmem_limit_bytes=40 * 2**20
        ),
        name="relay_backward",
    )(*flat)
    return grad_a.T[None], grad_b[None]


def solution(mesh):
    n, m = mesh.shape["pipe"], mesh.shape["dp"]
    row, part = P("pipe", "dp", None), P("dp", None)
    table = P("pipe", None, None)
    return jax.shard_map(
        functools.partial(per_device, n, m),
        mesh=mesh,
        in_specs=(row,) * 6 + (part,) * 2 + (table,) * 4,
        out_specs=(P("pipe", "dp", None), P("pipe", None, "dp")),
        check_vma=False,
    )
```

```python
import functools

import jax
import jax.numpy as jnp
from jax import lax
from jax.experimental import pallas as pl
from jax.experimental.pallas import tpu as pltpu
from jax.sharding import PartitionSpec as P

EPS = 1e-06
F32 = jnp.float32
BF16 = jnp.bfloat16


def dot_nt(a, b):
    return lax.dot_general(a, b, (((1,), (1,)), ((), ())), preferred_element_type=F32)


def dot_nn(a, b):
    return lax.dot_general(a, b, (((1,), (0,)), ((), ())), preferred_element_type=F32)


def dot_tn(a, b):
    return lax.dot_general(a, b, (((0,), (0,)), ((), ())), preferred_element_type=F32)


def kernel(
    n,
    m,
    kdf,
    kuf,
    kds,
    kus,
    cd,
    cu,
    ld,
    lu,
    sa,
    sb,
    ma,
    mb,
    ga,
    gb,
    x1,
    x2,
    g1,
    ls,
    wa,
    wb,
    nb,
    dxb,
    hs,
    hr,
    gs,
    gr,
    part,
    other,
    total,
    arrived,
    rs,
    rr,
    ms,
    mr,
    loc,
    snd,
    rcv,
):
    rows, width = x1.shape[1:]
    rank = wa.shape[1]
    chunk = width // m
    half = width // 2
    hm = m // 2
    tile = min(chunk, 768)
    tiles = width // tile
    per = chunk // tile
    factor = 1.0 / float(rows * m) ** 0.5

    j = lax.axis_index("pipe")
    d = lax.axis_index("dp")
    par = lax.rem(d, 2)
    kk = lax.div(d, 2)
    up = lax.rem(j + 1, n)
    down = lax.rem(j + n - 1, n)
    mirror = n - 1 - j
    pair = (j, d + 1 - 2 * par)
    ahead, behind, across = (up, d), (down, d), (mirror, d)

    def peer(q):
        return lax.rem(kk + q, hm)

    sources = (
        (kds, x2.at[0]),
        (sa, wa.at[0]),
        (kus, x2.at[1]),
        (ma, wa.at[1]),
        (kdf, x1.at[0]),
        (cd, g1.at[0]),
        (sb, wb.at[0]),
        (kuf, x1.at[1]),
        (cu, g1.at[1]),
        (mb, wb.at[1]),
    )
    loads = [
        pltpu.make_async_copy(src, dst, loc.at[at])
        for at, (src, dst) in enumerate(sources)
    ]

    barrier = pltpu.get_barrier_semaphore()
    greeted = [ahead, behind, across, pair]
    greeted += [(j, peer(q) * 2 + par) for q in range(1, hm)]
    for friend in greeted:
        pl.semaphore_signal(
            barrier, inc=1, device_id=friend, device_id_type=pl.DeviceIdType.MESH
        )
    for at in range(4):
        loads[at].start()
    pl.semaphore_wait(barrier, len(greeted))

    def send(slot, src, dst, target):
        copy = pltpu.make_async_remote_copy(
            src_ref=src,
            dst_ref=dst,
            send_sem=snd.at[slot],
            recv_sem=rcv.at[slot],
            device_id=target,
            device_id_type=pl.DeviceIdType.MESH,
        )
        copy.start()
        return copy

    mine = pl.ds(pl.multiple_of(par * half, 128), half)
    toward = (ahead, behind)
    back = (behind, ahead)
    halves = [
        send(w, src.at[:, mine], nb.at[w, par], toward[w])
        for w, src in enumerate((sb, mb))
    ]

    for at in range(4, 10):
        loads[at].start()
    edge = (j == 0, j == n - 1)
    losses = [
        pltpu.make_async_copy(src, ls, loc.at[10 + w]) for w, src in enumerate((ld, lu))
    ]
    for w in range(2):
        pl.when(edge[w])(losses[w].start)

    def cols(t):
        return pl.ds(pl.multiple_of(t * tile, 128), tile)

    def square_sum(x):
        xf = x.astype(F32)
        return jnp.sum(xf * xf, axis=-1, keepdims=True)

    def wide(x):
        return jnp.concatenate([x] * (128 // rank), axis=1)

    both = (0, 1)
    zero_r = jnp.zeros((rows, rank), F32)
    zero_1 = jnp.zeros((rows, 1), F32)

    def loop(body, start=0):
        return lax.fori_loop(0, tiles, body, start, unroll=2)

    for at in range(4):
        loads[at].wait()

    def forward(t, carry):
        after = []
        for w in both:
            ss, xa = carry[w]
            x = x2[w, :, cols(t)]
            after.append((ss + square_sum(x), xa + dot_nt(x, wa[w, :, cols(t)])))
        return tuple(after)

    inverse2, pre2 = [], []
    hidden_copies = []
    for w, (ss, xa) in enumerate(loop(forward, ((zero_1, zero_r),) * 2)):
        inv = lax.rsqrt(ss / width + EPS)
        pre = xa * inv
        inverse2.append(inv)
        pre2.append(pre)
        hs[w] = wide(pre * jax.nn.sigmoid(pre)).astype(BF16)
        hidden_copies.append(send(4 + w, hs.at[w], hr.at[w], toward[w]))

    for at in range(4, 10):
        loads[at].wait()

    def project(t, carry):
        after = []
        for w in both:
            ss, xa, gh = carry[w]
            x = x1[w, :, cols(t)]
            after.append(
                (
                    ss + square_sum(x),
                    xa + dot_nt(x, wa[w, :, cols(t)]),
                    gh + dot_nt(g1[w, :, cols(t)], wb[w, :, cols(t)]),
                )
            )
        return tuple(after)

    first = []
    for ss, xa, gh in loop(project, ((zero_1, zero_r, zero_r),) * 2):
        inv = lax.rsqrt(ss / width + EPS)
        pre = xa * inv
        sg = jax.nn.sigmoid(pre)
        h = (pre * sg).astype(BF16)
        dp = gh * sg * (1.0 + pre * (1.0 - sg))
        dpb = dp.astype(BF16)
        inner = jnp.sum(dpb.astype(F32) * pre, axis=-1, keepdims=True) / width
        first.append((inv, h, dpb, inv * inv * inner, (dp * inv).astype(BF16)))

    def place(t):
        k = lax.div(t, per)
        at = pl.ds(pl.multiple_of(lax.rem(t, per) * tile, 128), tile)
        return lax.rem(k, 2), lax.div(k, 2), at

    def send_half(g):
        return send(8 + g, part.at[g, 1 - par], other.at[g], pair)

    def send_quarters(g, copy):
        copy.wait_recv()
        copies = []
        for q in range(1, hm):
            k = peer(q)
            for i in range(2):
                total[g, k, i] = (
                    part[g, par, k, i].astype(F32) + other[g, k, i].astype(F32)
                ).astype(BF16)
            copies.append(
                send(
                    14 + g * (hm - 1) + q,
                    total.at[g, k],
                    arrived.at[g, q - 1],
                    (j, k * 2 + par),
                )
            )
        return copies

    def final(g, i):
        value = part[g, par, kk, i].astype(F32) + other[g, kk, i].astype(F32)
        for q in range(1, hm):
            value = value + arrived[g, q - 1, i].astype(F32)
        return value

    def grads_first(t, carry):
        odd, k, at = place(t)
        for w in both:
            value = dot_tn(first[w][1], g1[w, :, cols(t)])
            part[0, odd, k, w, :, at] = value.astype(BF16)
        return carry

    loop(grads_first)
    half_first = send_half(0)

    def cotangent(t, carry):
        for w in both:
            inv, h, dpb, scale, wdp = first[w]
            dx = (
                g1[w, :, cols(t)].astype(F32)
                + inv * dot_nn(dpb, wa[w, :, cols(t)])
                - x1[w, :, cols(t)].astype(F32) * scale
            )
            dxb[w, :, cols(t)] = dx.astype(BF16)
        return carry

    loop(cotangent)
    for w in both:

        @pl.when(edge[w])
        def _(w=w):
            losses[w].wait()

            def loss(t, carry):
                dxb[w, :, cols(t)] = ls[:, cols(t)]
                return carry

            lax.fori_loop(0, tiles, loss, 0)

    quarters = [send_quarters(0, half_first)]

    for copy in hidden_copies:
        copy.wait_recv()
    h_next = [hr[w][:, :rank] for w in both]

    def grads_second(t, carry):
        odd, k, at = place(t)
        for w in both:
            value = dot_tn(h_next[w], dxb[w, :, cols(t)])
            part[1, odd, k, w, :, at] = value.astype(BF16)
        return carry

    loop(grads_second)
    half_second = send_half(1)

    passed = []
    for w in both:
        halves[w].wait_recv()
        passed.append(send(2 + w, nb.at[w, par], nb.at[w, par], pair))
    quarters.append(send_quarters(1, half_second))

    for copy in passed:
        copy.wait_recv()

    def product(t, carry):
        side = lax.div(t, tiles // 2)
        at = cols(lax.rem(t, tiles // 2))
        return tuple(
            carry[w] + dot_nt(dxb[w, :, cols(t)], nb[w, side, :, at]) for w in both
        )

    returned = []
    for w, gh in enumerate(loop(product, (zero_r, zero_r))):
        gs[w] = wide(gh)
        returned.append(send(6 + w, gs.at[w], gr.at[w], back[w]))

    wdp2 = []
    for w in both:
        returned[w].wait_recv()
        pre = pre2[w]
        sg = jax.nn.sigmoid(pre)
        dp = gr[w][:, :rank] * sg * (1.0 + pre * (1.0 - sg))
        wdp2.append((dp * inverse2[w]).astype(BF16))

    def grads_a(t, carry):
        odd, k, at = place(t)
        for w in both:
            value = dot_tn(first[w][4], x1[w, :, cols(t)])
            value = value + dot_tn(wdp2[w], x2[w, :, cols(t)])
            part[2, odd, k, w, :, at] = value.astype(BF16)
        return carry

    loop(grads_a)
    half_a = send_half(2)

    quarters.append(send_quarters(2, half_a))

    for copy in quarters[1]:
        copy.wait_recv()
    rings = []
    for w in (1, 0):
        rs[w] = final(1, w).astype(BF16)
        rings.append(send(11 + w, rs.at[w], rr.at[w], back[w]))
    for copy in quarters[0]:
        copy.wait_recv()
    rings[0].wait_recv()
    ms[1] = (final(0, 1) + rr[1].astype(F32)).astype(BF16)
    mirror_b = send(14, ms.at[1], mr.at[1], across)
    for copy in quarters[2]:
        copy.wait_recv()
    ms[0] = final(2, 1).astype(BF16)
    mirror_a = send(13, ms.at[0], mr.at[0], across)
    rings[1].wait_recv()
    gb[...] = final(0, 0) + rr[0].astype(F32)
    ga[...] = final(2, 0)
    mirror_b.wait_recv()
    gb[...] = (gb[...] + mr[1].astype(F32)) * factor
    mirror_a.wait_recv()
    ga[...] = (ga[...] + mr[0].astype(F32)) * factor

    started = halves + passed + hidden_copies + returned + rings
    started += quarters[0] + quarters[1] + quarters[2]
    for copy in started + [half_first, half_second, half_a, mirror_a, mirror_b]:
        copy.wait_send()


def per_device(n, m, *args):
    flat = [a if a.ndim == 2 else a[0] for a in args]
    for at in (8, 10):
        flat[at] = flat[at].T
    rows, width = flat[0].shape
    rank = flat[8].shape[0]
    chunk = width // m
    hm = m // 2
    copies = 15 + 3 * (hm - 1)

    def vmem(*shape, dtype=BF16):
        return pltpu.VMEM(shape, dtype)

    grad_a, grad_b = pl.pallas_call(
        functools.partial(kernel, n, m),
        out_shape=[jax.ShapeDtypeStruct((rank, chunk), F32)] * 2,
        in_specs=[pl.BlockSpec(memory_space=pltpu.HBM)] * 12,
        out_specs=[pl.BlockSpec(memory_space=pltpu.VMEM)] * 2,
        scratch_shapes=[
            vmem(2, rows, width),
            vmem(2, rows, width),
            vmem(2, rows, width),
            vmem(rows, width),
            vmem(2, rank, width),
            vmem(2, rank, width),
            vmem(2, 2, rank, width // 2),
            vmem(2, rows, width),
            vmem(2, rows, 128),
            vmem(2, rows, 128),
            vmem(2, rows, 128, dtype=F32),
            vmem(2, rows, 128, dtype=F32),
            vmem(3, 2, hm, 2, rank, chunk),
            vmem(3, hm, 2, rank, chunk),
            vmem(3, hm, 2, rank, chunk),
            vmem(3, hm - 1, 2, rank, chunk),
            vmem(2, rank, chunk),
            vmem(2, rank, chunk),
            vmem(2, rank, chunk),
            vmem(2, rank, chunk),
            pltpu.SemaphoreType.DMA((12,)),
            pltpu.SemaphoreType.DMA((copies,)),
            pltpu.SemaphoreType.DMA((copies,)),
        ],
        compiler_params=pltpu.CompilerParams(
            collective_id=0, has_side_effects=True, vmem_limit_bytes=60 * 2**20
        ),
        name="relay_backward",
    )(*flat)
    return grad_a.T[None], grad_b[None]


def solution(mesh):
    n, m = mesh.shape["pipe"], mesh.shape["dp"]
    row, part = P("pipe", "dp", None), P("dp", None)
    table = P("pipe", None, None)
    return jax.shard_map(
        functools.partial(per_device, n, m),
        mesh=mesh,
        in_specs=(row,) * 6 + (part,) * 2 + (table,) * 4,
        out_specs=(P("pipe", "dp", None), P("pipe", None, "dp")),
        check_vma=False,
    )
```

```python
import functools

import jax
import jax.numpy as jnp
from jax import lax
from jax.experimental import pallas as pl
from jax.experimental.pallas import tpu as pltpu
from jax.sharding import PartitionSpec as P

EPS = 1e-06
F32 = jnp.float32
BF16 = jnp.bfloat16


def dot_nt(a, b):
    return lax.dot_general(a, b, (((1,), (1,)), ((), ())), preferred_element_type=F32)


def dot_nn(a, b):
    return lax.dot_general(a, b, (((1,), (0,)), ((), ())), preferred_element_type=F32)


def dot_tn(a, b):
    return lax.dot_general(a, b, (((0,), (0,)), ((), ())), preferred_element_type=F32)


def kernel(
    n,
    m,
    kdf,
    kuf,
    kds,
    kus,
    cd,
    cu,
    ld,
    lu,
    sa,
    sb,
    ma,
    mb,
    ga,
    gb,
    x1,
    x2,
    g1,
    ls,
    wa,
    wb,
    nb,
    dxb,
    hs,
    hr,
    gs,
    gr,
    part,
    other,
    total,
    arrived,
    rs,
    rr,
    ms,
    mr,
    loc,
    snd,
    rcv,
):
    rows, width = x1.shape[1:]
    rank = wa.shape[1]
    chunk = width // m
    half = width // 2
    hm = m // 2
    tile = min(chunk, 768)
    tiles = width // tile
    per = chunk // tile
    factor = 1.0 / float(rows * m) ** 0.5

    j = lax.axis_index("pipe")
    d = lax.axis_index("dp")
    par = lax.rem(d, 2)
    kk = lax.div(d, 2)
    up = lax.rem(j + 1, n)
    down = lax.rem(j + n - 1, n)
    mirror = n - 1 - j
    pair = (j, d + 1 - 2 * par)
    ahead, behind, across = (up, d), (down, d), (mirror, d)

    def peer(q):
        return lax.rem(kk + q, hm)

    sources = (
        (kds, x2.at[0]),
        (sa, wa.at[0]),
        (kus, x2.at[1]),
        (ma, wa.at[1]),
        (kdf, x1.at[0]),
        (cd, g1.at[0]),
        (sb, wb.at[0]),
        (kuf, x1.at[1]),
        (cu, g1.at[1]),
        (mb, wb.at[1]),
    )
    loads = [
        pltpu.make_async_copy(src, dst, loc.at[at])
        for at, (src, dst) in enumerate(sources)
    ]

    barrier = pltpu.get_barrier_semaphore()
    greeted = [ahead, behind, across, pair]
    greeted += [(j, peer(q) * 2 + par) for q in range(1, hm)]
    for friend in greeted:
        pl.semaphore_signal(
            barrier, inc=1, device_id=friend, device_id_type=pl.DeviceIdType.MESH
        )
    for at in range(4):
        loads[at].start()
    pl.semaphore_wait(barrier, len(greeted))

    def send(slot, src, dst, target):
        copy = pltpu.make_async_remote_copy(
            src_ref=src,
            dst_ref=dst,
            send_sem=snd.at[slot],
            recv_sem=rcv.at[slot],
            device_id=target,
            device_id_type=pl.DeviceIdType.MESH,
        )
        copy.start()
        return copy

    mine = pl.ds(pl.multiple_of(par * half, 128), half)
    toward = (ahead, behind)
    back = (behind, ahead)
    for at in range(4, 10):
        loads[at].start()
    edge = (j == 0, j == n - 1)
    losses = [
        pltpu.make_async_copy(src, ls, loc.at[10 + w]) for w, src in enumerate((ld, lu))
    ]
    for w in range(2):
        pl.when(edge[w])(losses[w].start)

    def cols(t):
        return pl.ds(pl.multiple_of(t * tile, 128), tile)

    def square_sum(x):
        xf = x.astype(F32)
        return jnp.sum(xf * xf, axis=-1, keepdims=True)

    def wide(x):
        return jnp.concatenate([x] * (128 // rank), axis=1)

    both = (0, 1)
    zero_r = jnp.zeros((rows, rank), F32)
    zero_1 = jnp.zeros((rows, 1), F32)

    def loop(body, start=0):
        return lax.fori_loop(0, tiles, body, start, unroll=4)

    for at in range(4):
        loads[at].wait()

    def forward(t, carry):
        after = []
        for w in both:
            ss, xa = carry[w]
            x = x2[w, :, cols(t)]
            after.append((ss + square_sum(x), xa + dot_nt(x, wa[w, :, cols(t)])))
        return tuple(after)

    inverse2, pre2 = [], []
    hidden_copies = []
    for w, (ss, xa) in enumerate(loop(forward, ((zero_1, zero_r),) * 2)):
        inv = lax.rsqrt(ss / width + EPS)
        pre = xa * inv
        inverse2.append(inv)
        pre2.append(pre)
        hs[w] = wide(pre * jax.nn.sigmoid(pre)).astype(BF16)
        hidden_copies.append(send(4 + w, hs.at[w], hr.at[w], toward[w]))

    halves = [
        send(w, src.at[:, mine], nb.at[w, par], toward[w])
        for w, src in enumerate((sb, mb))
    ]

    for at in range(4, 10):
        loads[at].wait()

    def project(t, carry):
        after = []
        for w in both:
            ss, xa, gh = carry[w]
            x = x1[w, :, cols(t)]
            after.append(
                (
                    ss + square_sum(x),
                    xa + dot_nt(x, wa[w, :, cols(t)]),
                    gh + dot_nt(g1[w, :, cols(t)], wb[w, :, cols(t)]),
                )
            )
        return tuple(after)

    first = []
    for ss, xa, gh in loop(project, ((zero_1, zero_r, zero_r),) * 2):
        inv = lax.rsqrt(ss / width + EPS)
        pre = xa * inv
        sg = jax.nn.sigmoid(pre)
        h = (pre * sg).astype(BF16)
        dp = gh * sg * (1.0 + pre * (1.0 - sg))
        dpb = dp.astype(BF16)
        inner = jnp.sum(dpb.astype(F32) * pre, axis=-1, keepdims=True) / width
        first.append((inv, h, dpb, inv * inv * inner, (dp * inv).astype(BF16)))

    def place(t):
        k = lax.div(t, per)
        at = pl.ds(pl.multiple_of(lax.rem(t, per) * tile, 128), tile)
        return lax.rem(k, 2), lax.div(k, 2), at

    def send_half(g):
        return send(8 + g, part.at[g, 1 - par], other.at[g], pair)

    def send_quarters(g, copy):
        copy.wait_recv()
        copies = ([], [])
        for i in (1, 0):
            for q in range(1, hm):
                k = peer(q)
                total[g, k, i] = (
                    part[g, par, k, i].astype(F32) + other[g, k, i].astype(F32)
                ).astype(BF16)
                copies[i].append(
                    send(
                        15 + (g * (hm - 1) + q - 1) * 2 + i,
                        total.at[g, k, i],
                        arrived.at[g, q - 1, i],
                        (j, k * 2 + par),
                    )
                )
        return copies

    def final(g, i):
        value = part[g, par, kk, i].astype(F32) + other[g, kk, i].astype(F32)
        for q in range(1, hm):
            value = value + arrived[g, q - 1, i].astype(F32)
        return value

    def grads_first(t, carry):
        odd, k, at = place(t)
        for w in both:
            value = dot_tn(first[w][1], g1[w, :, cols(t)])
            part[0, odd, k, w, :, at] = value.astype(BF16)
        return carry

    loop(grads_first)
    half_first = send_half(0)

    def cotangent(t, carry):
        for w in both:
            inv, h, dpb, scale, wdp = first[w]
            dx = (
                g1[w, :, cols(t)].astype(F32)
                + inv * dot_nn(dpb, wa[w, :, cols(t)])
                - x1[w, :, cols(t)].astype(F32) * scale
            )
            dxb[w, :, cols(t)] = dx.astype(BF16)
        return carry

    loop(cotangent)
    for w in both:

        @pl.when(edge[w])
        def _(w=w):
            losses[w].wait()

            def loss(t, carry):
                dxb[w, :, cols(t)] = ls[:, cols(t)]
                return carry

            lax.fori_loop(0, tiles, loss, 0)

    quarters = [send_quarters(0, half_first)]

    for copy in hidden_copies:
        copy.wait_recv()
    h_next = [hr[w][:, :rank] for w in both]

    def grads_second(t, carry):
        odd, k, at = place(t)
        for w in both:
            value = dot_tn(h_next[w], dxb[w, :, cols(t)])
            part[1, odd, k, w, :, at] = value.astype(BF16)
        return carry

    loop(grads_second)
    half_second = send_half(1)

    passed = []
    for w in both:
        halves[w].wait_recv()
        passed.append(send(2 + w, nb.at[w, par], nb.at[w, par], pair))

    for copy in passed:
        copy.wait_recv()

    def product(t, carry):
        side = lax.div(t, tiles // 2)
        at = cols(lax.rem(t, tiles // 2))
        return tuple(
            carry[w] + dot_nt(dxb[w, :, cols(t)], nb[w, side, :, at]) for w in both
        )

    returned = []
    for w, gh in enumerate(loop(product, (zero_r, zero_r))):
        gs[w] = wide(gh)
        returned.append(send(6 + w, gs.at[w], gr.at[w], back[w]))

    quarters.append(send_quarters(1, half_second))
    wdp2 = []
    for w in both:
        returned[w].wait_recv()
        pre = pre2[w]
        sg = jax.nn.sigmoid(pre)
        dp = gr[w][:, :rank] * sg * (1.0 + pre * (1.0 - sg))
        wdp2.append((dp * inverse2[w]).astype(BF16))

    def grads_a(t, carry):
        odd, k, at = place(t)
        for w in both:
            value = dot_tn(first[w][4], x1[w, :, cols(t)])
            value = value + dot_tn(wdp2[w], x2[w, :, cols(t)])
            part[2, odd, k, w, :, at] = value.astype(BF16)
        return carry

    loop(grads_a)
    half_a = send_half(2)

    quarters.append(send_quarters(2, half_a))

    def arrive(g, i):
        for copy in quarters[g][i]:
            copy.wait_recv()

    rings = []
    for w in (1, 0):
        arrive(1, w)
        rs[w] = final(1, w).astype(BF16)
        rings.append(send(11 + w, rs.at[w], rr.at[w], back[w]))
    arrive(0, 1)
    rings[0].wait_recv()
    ms[1] = (final(0, 1) + rr[1].astype(F32)).astype(BF16)
    mirror_b = send(14, ms.at[1], mr.at[1], across)
    arrive(2, 1)
    ms[0] = final(2, 1).astype(BF16)
    mirror_a = send(13, ms.at[0], mr.at[0], across)
    arrive(0, 0)
    rings[1].wait_recv()
    gb[...] = final(0, 0) + rr[0].astype(F32)
    arrive(2, 0)
    ga[...] = final(2, 0)
    mirror_b.wait_recv()
    gb[...] = (gb[...] + mr[1].astype(F32)) * factor
    mirror_a.wait_recv()
    ga[...] = (ga[...] + mr[0].astype(F32)) * factor

    started = halves + passed + hidden_copies + returned + rings
    for lists in quarters:
        started += lists[0] + lists[1]
    for copy in started + [half_first, half_second, half_a, mirror_a, mirror_b]:
        copy.wait_send()


def per_device(n, m, *args):
    flat = [a if a.ndim == 2 else a[0] for a in args]
    for at in (8, 10):
        flat[at] = flat[at].T
    rows, width = flat[0].shape
    rank = flat[8].shape[0]
    chunk = width // m
    hm = m // 2
    copies = 15 + 6 * (hm - 1)

    def vmem(*shape, dtype=BF16):
        return pltpu.VMEM(shape, dtype)

    grad_a, grad_b = pl.pallas_call(
        functools.partial(kernel, n, m),
        out_shape=[jax.ShapeDtypeStruct((rank, chunk), F32)] * 2,
        in_specs=[pl.BlockSpec(memory_space=pltpu.HBM)] * 12,
        out_specs=[pl.BlockSpec(memory_space=pltpu.VMEM)] * 2,
        scratch_shapes=[
            vmem(2, rows, width),
            vmem(2, rows, width),
            vmem(2, rows, width),
            vmem(rows, width),
            vmem(2, rank, width),
            vmem(2, rank, width),
            vmem(2, 2, rank, width // 2),
            vmem(2, rows, width),
            vmem(2, rows, 128),
            vmem(2, rows, 128),
            vmem(2, rows, 128, dtype=F32),
            vmem(2, rows, 128, dtype=F32),
            vmem(3, 2, hm, 2, rank, chunk),
            vmem(3, hm, 2, rank, chunk),
            vmem(3, hm, 2, rank, chunk),
            vmem(3, hm - 1, 2, rank, chunk),
            vmem(2, rank, chunk),
            vmem(2, rank, chunk),
            vmem(2, rank, chunk),
            vmem(2, rank, chunk),
            pltpu.SemaphoreType.DMA((12,)),
            pltpu.SemaphoreType.DMA((copies,)),
            pltpu.SemaphoreType.DMA((copies,)),
        ],
        compiler_params=pltpu.CompilerParams(
            collective_id=0, has_side_effects=True, vmem_limit_bytes=60 * 2**20
        ),
        name="relay_backward",
    )(*flat)
    return grad_a.T[None], grad_b[None]


def solution(mesh):
    n, m = mesh.shape["pipe"], mesh.shape["dp"]
    row, part = P("pipe", "dp", None), P("dp", None)
    table = P("pipe", None, None)
    return jax.shard_map(
        functools.partial(per_device, n, m),
        mesh=mesh,
        in_specs=(row,) * 6 + (part,) * 2 + (table,) * 4,
        out_specs=(P("pipe", "dp", None), P("pipe", None, "dp")),
        check_vma=False,
    )
```
